512 devices in a mesh: blk: 64 (over z_hi, y, core), head: 8 (over x, z_lo).
Axes of the slice: x: 4, y: 8, z: 8 (z_hi: 4, z_lo: 2; z = z_hi * 2 + z_lo), core: 2. Of those that a mesh axis runs over, the one named last changes fastest.
Arguments:
- queries: bfloat16 [65536, 2048], P(('blk', 'head')), may hold values from -20 to 20
- keys: bfloat16 [65536, 1024], P(('blk', 'head')), may hold values from -20 to 20
- values: bfloat16 [65536, 1024], P(('blk', 'head')), may hold values from -6 to 6
- outputs: bfloat16 [65536, 2048], P(('blk', 'head')), may hold values from -6 to 6
- out_grads: bfloat16 [65536, 2048], P(('blk', 'head')), may hold values from -6 to 6
- segment_ids: int32 [65536], replicated, may hold values from 0 to 255, never falling along the last dimension, each value on 1 to 512 neighbouring positions
- block_order: int32 [128], replicated, may hold values from 0 to 127, as said below
Outputs:
- query_grads: bfloat16 [65536, 2048], P(('blk', 'head'))
- key_grads: bfloat16 [65536, 1024], P(('blk', 'head'))
- value_grads: bfloat16 [65536, 1024], P(('blk', 'head'))
The draws below stay inside these ranges and needn't reach their ends.
Inputs may be any that keep to these rules, and one draw needn't show every extreme that they name: `segment_ids`: never falling along the sequence; each document has 1 to 512 tokens, one exactly 512. `block_order`: slots 2 i and 2 i + 1 hold the half-blocks i and 127 - i, in either order.
All inputs are finite; a program needn't handle non-finite values.
Results may differ from the reference program's by a relative error of at most 0.008.
Values may be sent and summed in bfloat16 or wider, within the bound.
A program may use at most 64 MiB of HBM per device.

```python
import math
import jax
import jax.numpy as jnp
import numpy as np
from jax import lax

QUERY_HEADS = 16
KEY_VALUE_HEADS = 8
HEAD_SIZE = 128
PACKED_TOKENS = 65536
HALF = 512
HALVES = 128
DOCS = 256
DOC_MOST = 512


def key_base(key):
    return jnp.clip(jax.random.normal(key, (PACKED_TOKENS, KEY_VALUE_HEADS * HEAD_SIZE), jnp.float32), -6.0, 6.0)


def draw_keys(key, part):
    base = key_base(key)
    result = base
    return result.astype(jnp.bfloat16)


def draw_queries(key, part):
    key = jax.random.fold_in(key, 12)
    own = jnp.clip(jax.random.normal(key, (PACKED_TOKENS, QUERY_HEADS * HEAD_SIZE), jnp.float32), -6.0, 6.0)
    result = own
    return result.astype(jnp.bfloat16)


def draw_block_order(key, part):
    key = jax.random.fold_in(key, 13)
    pair_count = HALVES // 2
    early_half = jnp.arange(pair_count, dtype=jnp.int32)
    late_half = (HALVES - 1 - early_half).astype(jnp.int32)
    flipped = jax.random.randint(key, (pair_count,), 0, 2, dtype=jnp.int32)
    slot_low = jnp.where(flipped == 1, late_half, early_half)
    slot_high = jnp.where(flipped == 1, early_half, late_half)
    return jnp.stack([slot_low, slot_high], axis=1).reshape(HALVES).astype(jnp.int32)


def shard_levels(key, dims, pieces, smallest, high):
    loudness = 1.0
    for position, blocks in pieces:
        draws = jax.random.uniform(jax.random.fold_in(jax.random.fold_in(key, 6), position), (blocks,), jnp.float32, smallest / len(pieces), high / len(pieces))
        loudness = loudness * jnp.repeat(jnp.exp(draws), dims[position] // blocks).reshape((-1,) + (1,) * (len(dims) - 1 - position))
    return loudness


def length_profile(number_of, total, reach, slope):
    loads = [(1 << 20) // math.isqrt(grade ** slope) + 1 for grade in range(2, number_of + 1)]
    surplus, given = total - reach - (number_of - 1), [1] * (number_of - 1)
    while surplus > 0:
        movable = [i for i in range(number_of - 1) if given[i] < reach]
        mass, remaining = sum([loads[i] for i in movable]), surplus
        for i in movable:
            more = min(reach - given[i], max(1, remaining * loads[i] // mass), surplus)
            given[i] = given[i] + more
            surplus = surplus - more
    return np.array([reach] + given)


def ragged_sizes(own_key, count, total, bound, lean):
    if count == 2:
        one = jax.random.randint(own_key, (), max(1, total - bound), min(bound, total - 1) + 1)
        return jnp.stack([one, total - one])
    tallies = jnp.asarray(length_profile(count, total, bound, lean), jnp.int32)
    twos = (count - 1) // 2
    source_of, receiver = tallies[1:1 + 2 * twos:2], tallies[2:2 + 2 * twos:2]
    slack = jnp.minimum(source_of - 1, bound - receiver)
    shifted = jax.random.randint(jax.random.fold_in(own_key, 1), (twos,), 0, 1 << 20) % (slack + 1)
    tallies = tallies.at[1:1 + 2 * twos:2].set(source_of - shifted).at[2:2 + 2 * twos:2].set(receiver + shifted)
    return tallies[jax.random.permutation(jax.random.fold_in(own_key, 2), count)]


def scatter_about(key, dims, width, most, pieces=(), held_as=jnp.bfloat16):
    level = shard_levels(key, dims, pieces, -0.22, 0.18) if pieces else 1.0
    entries = jax.random.normal(key, dims, jnp.float32) * width * level
    return jnp.minimum(jnp.maximum(entries, -most), most).astype(held_as)


def setup_inputs(seed: int = 0) -> dict:
    key_of = jax.random.split(jax.random.key(seed), 8)
    return {
        "queries": draw_queries(jax.random.fold_in(key_of[7], 71), 0),
        "keys": draw_keys(jax.random.fold_in(key_of[7], 71), 0),
        "values": scatter_about(key_of[2], (PACKED_TOKENS, KEY_VALUE_HEADS * HEAD_SIZE), 1.0, 6.0, ((0, 512),)),
        "outputs": scatter_about(key_of[3], (PACKED_TOKENS, QUERY_HEADS * HEAD_SIZE), 1.0, 6.0, ((0, 512),)),
        "out_grads": scatter_about(key_of[4], (PACKED_TOKENS, QUERY_HEADS * HEAD_SIZE), 1.0, 6.0, ((0, 512),)),
        "segment_ids": jnp.searchsorted(jnp.cumsum(ragged_sizes(key_of[5], DOCS, PACKED_TOKENS, DOC_MOST, 2)), jnp.arange(PACKED_TOKENS), side="right").astype(jnp.int32),
        "block_order": draw_block_order(jax.random.fold_in(key_of[7], 71), 0),
    }


NEGATIVE = -1e30


def reference(queries, keys, values, outputs, out_grads, segment_ids, block_order):
    softmax_scale = HEAD_SIZE ** -0.5
    query_group_size = QUERY_HEADS // KEY_VALUE_HEADS
    stored = jnp.arange(PACKED_TOKENS, dtype=jnp.int32)
    positions = (block_order[stored // HALF] * HALF + stored % HALF).astype(jnp.int32)
    order = jnp.zeros((PACKED_TOKENS,), jnp.int32).at[positions].set(stored)
    seq_queries = queries[order]
    seq_keys = keys[order]
    seq_values = values[order]
    seq_outputs = outputs[order]
    seq_grads = out_grads[order]
    documents = segment_ids
    block = math.gcd(PACKED_TOKENS, 512)
    count = PACKED_TOKENS // block
    window = min(PACKED_TOKENS, DOC_MOST + block)
    query_parts = []
    key_parts = []
    value_parts = []
    for key_value_head in range(KEY_VALUE_HEADS):
        key_head = seq_keys[:, key_value_head * HEAD_SIZE:(key_value_head + 1) * HEAD_SIZE]
        value_head = seq_values[:, key_value_head * HEAD_SIZE:(key_value_head + 1) * HEAD_SIZE]
        key_acc = jnp.zeros((PACKED_TOKENS, HEAD_SIZE), jnp.float32)
        value_acc = jnp.zeros((PACKED_TOKENS, HEAD_SIZE), jnp.float32)
        for member in range(query_group_size):
            head = key_value_head * query_group_size + member
            query_head = seq_queries[:, head * HEAD_SIZE:(head + 1) * HEAD_SIZE]
            grad_head = seq_grads[:, head * HEAD_SIZE:(head + 1) * HEAD_SIZE]
            output_head = seq_outputs[:, head * HEAD_SIZE:(head + 1) * HEAD_SIZE]

            def one_block(carry, index):
                key_sum, value_sum = carry
                start = (index * block).astype(jnp.int32)
                win_start = jnp.clip(start - DOC_MOST, 0, PACKED_TOKENS - window).astype(jnp.int32)
                query_block = lax.dynamic_slice_in_dim(query_head, start, block, 0)
                grad_block = lax.dynamic_slice_in_dim(grad_head, start, block, 0)
                output_block = lax.dynamic_slice_in_dim(output_head, start, block, 0)
                key_win = lax.dynamic_slice_in_dim(key_head, win_start, window, 0)
                value_win = lax.dynamic_slice_in_dim(value_head, win_start, window, 0)
                pos_block = (start + jnp.arange(block, dtype=jnp.int32)).astype(jnp.int32)
                pos_win = (win_start + jnp.arange(window, dtype=jnp.int32)).astype(jnp.int32)
                doc_block = lax.dynamic_slice_in_dim(documents, start, block, 0)
                doc_win = lax.dynamic_slice_in_dim(documents, win_start, window, 0)
                visible = (doc_block[:, None] == doc_win[None, :]) & (pos_win[None, :] <= pos_block[:, None])
                raw = jnp.dot(query_block, key_win.T, preferred_element_type=jnp.float32) * softmax_scale
                scores = jnp.where(visible, raw, NEGATIVE)
                maxima = jnp.max(scores, axis=1)
                totals = jnp.sum(jnp.where(visible, jnp.exp(scores - maxima[:, None]), 0.0), axis=1)
                log_sums = maxima + jnp.log(totals)
                weights = jnp.where(visible, jnp.exp(scores - log_sums[:, None]), 0.0)
                weights_b = weights.astype(jnp.bfloat16)
                delta = jnp.sum(grad_block.astype(jnp.float32) * output_block.astype(jnp.float32), axis=1)
                weight_grads = jnp.dot(grad_block, value_win.T, preferred_element_type=jnp.float32)
                score_grads = weights * (weight_grads - delta[:, None])
                score_grads_b = score_grads.astype(jnp.bfloat16)
                query_block_grad = (jnp.dot(score_grads_b, key_win, preferred_element_type=jnp.float32) * softmax_scale).astype(jnp.bfloat16)
                key_term = jnp.dot(score_grads_b.T, query_block, preferred_element_type=jnp.float32)
                value_term = jnp.dot(weights_b.T, grad_block, preferred_element_type=jnp.float32)
                key_now = lax.dynamic_slice_in_dim(key_sum, win_start, window, 0)
                value_now = lax.dynamic_slice_in_dim(value_sum, win_start, window, 0)
                key_sum = lax.dynamic_update_slice_in_dim(key_sum, key_now + key_term, win_start, 0)
                value_sum = lax.dynamic_update_slice_in_dim(value_sum, value_now + value_term, win_start, 0)
                return (key_sum, value_sum), query_block_grad

            (key_acc, value_acc), query_blocks = lax.scan(one_block, (key_acc, value_acc), jnp.arange(count, dtype=jnp.int32))
            query_parts.append(query_blocks.reshape(PACKED_TOKENS, HEAD_SIZE))
        key_parts.append((key_acc * softmax_scale).astype(jnp.bfloat16))
        value_parts.append(value_acc.astype(jnp.bfloat16))
    query_seq = jnp.concatenate(query_parts, axis=1)
    key_seq = jnp.concatenate(key_parts, axis=1)
    value_seq = jnp.concatenate(value_parts, axis=1)
    return (query_seq[positions], key_seq[positions], value_seq[positions])
```

```python
import functools

import jax
import jax.numpy as jnp
from jax import lax
from jax.experimental import pallas as pl
from jax.experimental.pallas import tpu as pltpu
from jax.sharding import PartitionSpec as P

HEAD = 128
CHUNK = 128
HALF = 512
WINDOW = HALF + CHUNK
GROUPS = 8
SCALE = HEAD ** -0.5
LOG2E = 1.4426950408889634
HIDDEN = -1e30
MESH = pl.DeviceIdType.MESH
BF16 = jnp.bfloat16
F32 = jnp.float32
NT = (((1,), (1,)), ((), ()))
KINDS = 5


def kernel(
    q_hbm, k_hbm, v_hbm, o_hbm, g_hbm, seg, order,
    dq_out, dk_out, dv_out,
    q_all, g_all, k_all, v_all, kt_all, d_all, d_mine, o_rows, g_rows,
    halo, back, dk_sum, dv_sum, dq_stage, dk_stage, dv_stage, bias,
    load_sem, own_sem, in_send, in_recv, halo_send, halo_recv, back_send, back_recv,
    out_send, out_recv, out_own,
):
    i = lax.axis_index("blk")
    h = lax.axis_index("head")
    blocks = lax.axis_size("blk")
    x, z = h // 2, h % 2
    above = lax.rem(i + 1, blocks)
    below = lax.rem(i + blocks - 1, blocks)
    partners = [
        lax.rem(x + dx, 4) * 2 + lax.rem(z + dz, 2)
        for dx in (2, 1, 3, 0)
        for dz in (1, 0)
        if dx or dz
    ]

    barrier = pltpu.get_barrier_semaphore()
    for o in partners:
        pl.semaphore_signal(barrier, inc=1, device_id=(i, o), device_id_type=MESH)
    for b in (above, below):
        pl.semaphore_signal(barrier, inc=1, device_id=(b, h), device_id_type=MESH)

    loads = [
        pltpu.make_async_copy(o_hbm, o_rows, load_sem.at[0]),
        pltpu.make_async_copy(g_hbm, g_rows, load_sem.at[1]),
    ]
    for c in loads:
        c.start()

    def own_rows(o):
        return o // 4, pl.multiple_of(HALF + lax.rem(o, 4) * CHUNK, CHUNK)

    def cols(o, width):
        return pl.ds(pl.multiple_of(o * width, width), width)

    def piece(kind, target, source):
        s, row = own_rows(source)
        if kind == 0:
            return k_hbm.at[:, cols(target, HEAD)], k_all.at[s, pl.ds(row, CHUNK), :]
        if kind == 1:
            return v_hbm.at[:, cols(target, HEAD)], v_all.at[s, pl.ds(row, CHUNK), :]
        if kind == 2:
            return d_mine.at[target], d_all.at[source]
        if kind == 3:
            return q_hbm.at[:, cols(target, 2 * HEAD)], q_all.at[source]
        return g_hbm.at[:, cols(target, 2 * HEAD)], g_all.at[source]

    def send(kind, o):
        src, dst = piece(kind, o, h)
        return pltpu.make_async_remote_copy(
            src, dst, in_send.at[kind, o], in_recv.at[kind, h],
            device_id=(i, o), device_id_type=MESH,
        )

    def arrival(kind, o):
        src, dst = piece(kind, h, o)
        return pltpu.make_async_remote_copy(
            src, dst, in_send.at[kind, o], in_recv.at[kind, o],
            device_id=(i, o), device_id_type=MESH,
        )

    def own(kind):
        src, dst = piece(kind, h, h)
        return pltpu.make_async_copy(src, dst, own_sem.at[kind])

    for c in loads:
        c.wait()
    d_mine[...] = jnp.zeros_like(d_mine)
    for head in range(2 * GROUPS):
        at = slice(head * HEAD, (head + 1) * HEAD)
        product = o_rows[:, at].astype(F32) * g_rows[:, at].astype(F32)
        d_mine[head // 2, head % 2 : head % 2 + 1, :] = jnp.sum(
            product.T, axis=0, keepdims=True
        )

    pl.semaphore_wait(barrier, GROUPS + 1)
    for kind in range(KINDS):
        for o in partners:
            send(kind, o).start()
        own(kind).start()

    slot_half = [order[2 * i], order[2 * i + 1]]
    early = (slot_half[0] > slot_half[1]).astype(jnp.int32)
    is_early = [early == 0, early == 1]
    key_at = lax.broadcasted_iota(jnp.int32, (CHUNK, CHUNK), 0)
    row_at = lax.broadcasted_iota(jnp.int32, (CHUNK, CHUNK), 1)
    causal = key_at <= row_at
    for s in range(2):
        first = slot_half[s] * 4
        documents = []
        for c in range(8):
            line = seg[pl.ds(jnp.maximum(first - 4 + c, 0), 1), :].astype(F32)
            if c < 4:
                line = jnp.where(first == 0, -1.0, line)
            documents.append(line)
        for c in range(8):
            column = jnp.broadcast_to(documents[c], (CHUNK, CHUNK)).T
            for p in range(4):
                r = c - p
                if 0 <= r <= 4:
                    visible = column == documents[4 + p]
                    if r == 4:
                        visible = visible & causal
                    bias[s, p, r * CHUNK : (r + 1) * CHUNK, :] = jnp.where(
                        visible, 0.0, HIDDEN
                    )
    dk_sum[...] = jnp.zeros_like(dk_sum)
    dv_sum[...] = jnp.zeros_like(dv_sum)

    for kind in (0, 1):
        for o in partners:
            arrival(kind, o).wait_recv()
        own(kind).wait()
    late = 1 - early
    for n, slot in ((2, early), (3, late)):
        halo[n, 0] = k_all[slot, HALF:, :]
        halo[n, 1] = v_all[slot, HALF:, :]
    halo_up = pltpu.make_async_remote_copy(
        halo.at[2], halo.at[0], halo_send.at[0], halo_recv.at[0],
        device_id=(above, h), device_id_type=MESH,
    )
    halo_down = pltpu.make_async_remote_copy(
        halo.at[3], halo.at[1], halo_send.at[1], halo_recv.at[1],
        device_id=(below, h), device_id_type=MESH,
    )
    halo_up.start()
    halo_down.start()
    for s in range(2):
        kt_all[s, :, HALF:] = k_all[s, HALF:, :].T
    halo_up.wait_recv()
    halo_down.wait_recv()
    for s in range(2):
        at = jnp.where(is_early[s], 0, jnp.where(i == blocks - 1, 2, 1))
        before = halo[at, 0]
        k_all[s, :HALF, :] = before
        kt_all[s, :, :HALF] = before.T
        v_all[s, :HALF, :] = halo[at, 1]

    for kind in (2, 3, 4):
        for o in partners:
            arrival(kind, o).wait_recv()
        own(kind).wait()

    def out_piece(kind, target, source):
        if kind == 0:
            return dq_stage.at[target], dq_out.at[:, cols(source, 2 * HEAD)]
        if kind == 1:
            return dk_stage.at[target], dk_out.at[:, cols(source, HEAD)]
        return dv_stage.at[target], dv_out.at[:, cols(source, HEAD)]

    def out_remote(kind, target, source, o):
        src, dst = out_piece(kind, target, source)
        return pltpu.make_async_remote_copy(
            src, dst, out_send.at[kind, target], out_recv.at[kind, source],
            device_id=(i, o), device_id_type=MESH,
        )

    def out_local(kind):
        src, dst = out_piece(kind, h, h)
        return pltpu.make_async_copy(src, dst, out_own.at[kind])

    def give(kind, o):
        @pl.when(o != h)
        def _():
            out_remote(kind, o, h, o).start()

        @pl.when(o == h)
        def _():
            out_local(kind).start()

    def tile(s, p):
        o = s * 4 + p
        keys_at = pl.ds(pl.multiple_of(p * CHUNK, CHUNK), WINDOW)
        keys = k_all[s, keys_at, :]
        vals = v_all[s, keys_at, :]
        q_two = jnp.concatenate([q_all[o, :, :HEAD], q_all[o, :, HEAD:]], axis=0)
        g_two = jnp.concatenate([g_all[o, :, :HEAD], g_all[o, :, HEAD:]], axis=0)
        delta = jnp.concatenate([d_all[o, 0:1, :], d_all[o, 1:2, :]], axis=1)
        hide = bias[s, p]
        scores = lax.dot_general(keys, q_two, NT, preferred_element_type=F32)
        scores = scores * (SCALE * LOG2E) + jnp.concatenate([hide, hide], axis=1)
        top = jnp.max(scores, axis=0, keepdims=True)
        terms = jnp.exp2(scores - top)
        weights = terms * (1.0 / jnp.sum(terms, axis=0, keepdims=True))
        weights_b = weights.astype(BF16)
        pulls = lax.dot_general(vals, g_two, NT, preferred_element_type=F32)
        score_grads = (weights * (pulls - delta)).astype(BF16)
        dv_sum[s, keys_at, :] += jnp.dot(weights_b, g_two, preferred_element_type=F32)
        dk_sum[s, keys_at, :] += jnp.dot(score_grads, q_two, preferred_element_type=F32)
        dq = jnp.dot(kt_all[s, :, keys_at], score_grads, preferred_element_type=F32) * SCALE
        dq_stage[o, :, :HEAD] = dq[:, :HEAD].T.astype(BF16)
        dq_stage[o, :, HEAD:] = dq[:, HEAD:].T.astype(BF16)

    def step(d, carry):
        p = lax.rem(h + 1 + d, 4)
        for s in range(2):
            tile(s, p)
        for s in range(2):
            give(0, s * 4 + p)
        return carry

    lax.fori_loop(0, 4, step, 0)

    for n, slot in ((2, early), (3, late)):
        back[n, 0] = dk_sum[slot, :HALF, :].astype(BF16)
        back[n, 1] = dv_sum[slot, :HALF, :].astype(BF16)
    back_down = pltpu.make_async_remote_copy(
        back.at[2], back.at[1], back_send.at[0], back_recv.at[0],
        device_id=(below, h), device_id_type=MESH,
    )
    back_up = pltpu.make_async_remote_copy(
        back.at[3], back.at[0], back_send.at[1], back_recv.at[1],
        device_id=(above, h), device_id_type=MESH,
    )
    back_down.start()
    back_up.start()
    back_down.wait_recv()
    back_up.wait_recv()
    for s in range(2):
        at = jnp.where(is_early[s], jnp.where(i == blocks - 1, 3, 1), 0)
        nothing = jnp.logical_and(jnp.logical_not(is_early[s]), i == 0)
        for p in range(4):
            own_at = slice(HALF + p * CHUNK, HALF + (p + 1) * CHUNK)
            rows = slice(p * CHUNK, (p + 1) * CHUNK)
            dk_more = jnp.where(nothing, 0.0, back[at, 0, rows, :].astype(F32))
            dv_more = jnp.where(nothing, 0.0, back[at, 1, rows, :].astype(F32))
            dk_stage[s * 4 + p] = ((dk_sum[s, own_at, :] + dk_more) * SCALE).astype(BF16)
            dv_stage[s * 4 + p] = (dv_sum[s, own_at, :] + dv_more).astype(BF16)
    for kind in (1, 2):
        for o in partners:
            out_remote(kind, o, h, o).start()
        out_local(kind).start()

    halo_up.wait_send()
    halo_down.wait_send()
    back_down.wait_send()
    back_up.wait_send()
    for kind in range(KINDS):
        for o in partners:
            send(kind, o).wait_send()
    for kind in range(3):
        for o in partners:
            out_remote(kind, o, h, o).wait_send()
            out_remote(kind, h, o, o).wait_recv()
        out_local(kind).wait()


def local(queries, keys, values, outputs, out_grads, segment_ids, block_order):
    rows = queries.shape[0]
    hbm = pl.BlockSpec(memory_space=pl.ANY)
    vmem = pl.BlockSpec(memory_space=pltpu.VMEM)
    smem = pl.BlockSpec(memory_space=pltpu.SMEM)
    dma = pltpu.SemaphoreType.DMA
    return pl.pallas_call(
        kernel,
        out_shape=[
            jax.ShapeDtypeStruct((rows, queries.shape[1]), BF16),
            jax.ShapeDtypeStruct((rows, keys.shape[1]), BF16),
            jax.ShapeDtypeStruct((rows, values.shape[1]), BF16),
        ],
        in_specs=[hbm] * 5 + [vmem, smem],
        out_specs=[hbm] * 3,
        scratch_shapes=[
            pltpu.VMEM((GROUPS, CHUNK, 2 * HEAD), BF16),
            pltpu.VMEM((GROUPS, CHUNK, 2 * HEAD), BF16),
            pltpu.VMEM((2, 2 * HALF, HEAD), BF16),
            pltpu.VMEM((2, 2 * HALF, HEAD), BF16),
            pltpu.VMEM((2, HEAD, 2 * HALF), BF16),
            pltpu.VMEM((GROUPS, 8, CHUNK), F32),
            pltpu.VMEM((GROUPS, 8, CHUNK), F32),
            pltpu.VMEM((CHUNK, 2 * GROUPS * HEAD), BF16),
            pltpu.VMEM((CHUNK, 2 * GROUPS * HEAD), BF16),
            pltpu.VMEM((4, 2, HALF, HEAD), BF16),
            pltpu.VMEM((4, 2, HALF, HEAD), BF16),
            pltpu.VMEM((2, 2 * HALF, HEAD), F32),
            pltpu.VMEM((2, 2 * HALF, HEAD), F32),
            pltpu.VMEM((GROUPS, CHUNK, 2 * HEAD), BF16),
            pltpu.VMEM((GROUPS, CHUNK, HEAD), BF16),
            pltpu.VMEM((GROUPS, CHUNK, HEAD), BF16),
            pltpu.VMEM((2, 4, WINDOW, CHUNK), F32),
            dma((2,)),
            dma((KINDS,)),
            dma((KINDS, GROUPS)),
            dma((KINDS, GROUPS)),
            dma((2,)),
            dma((2,)),
            dma((2,)),
            dma((2,)),
            dma((3, GROUPS)),
            dma((3, GROUPS)),
            dma((3,)),
        ],
        compiler_params=pltpu.CompilerParams(
            collective_id=0, has_side_effects=True, vmem_limit_bytes=40 * 1024 * 1024
        ),
        name="attention_backward",
    )(
        queries, keys, values, outputs, out_grads,
        segment_ids.reshape(-1, CHUNK), block_order,
    )


def solution(mesh):
    row = P(("blk", "head"), None)
    return jax.shard_map(
        local,
        mesh=mesh,
        in_specs=(row,) * 5 + (P(), P()),
        out_specs=(row,) * 3,
        check_vma=False,
    )
```

```python
import functools

import jax
import jax.numpy as jnp
from jax import lax
from jax.experimental import pallas as pl
from jax.experimental.pallas import tpu as pltpu
from jax.sharding import PartitionSpec as P

HEAD = 128
CHUNK = 128
HALF = 512
WINDOW = HALF + CHUNK
GROUPS = 8
SCALE = HEAD ** -0.5
LOG2E = 1.4426950408889634
HIDDEN = -1e30
MESH = pl.DeviceIdType.MESH
BF16 = jnp.bfloat16
F32 = jnp.float32
NT = (((1,), (1,)), ((), ()))
KINDS = 5


def kernel(
    q_hbm, k_hbm, v_hbm, o_hbm, g_hbm, seg_hbm, order_hbm,
    dq_out, dk_out, dv_out,
    seg, order, q_all, g_all, k_all, v_all, kt_all, d_all, d_mine, o_rows, g_rows,
    q_two, g_two, w_all, s_all,
    halo, back, dk_sum, dv_sum, dq_stage, dk_stage, dv_stage, bias,
    load_sem, own_sem, in_send, in_recv, halo_send, halo_recv, back_send, back_recv,
    out_send, out_recv, out_own,
):
    i = lax.axis_index("blk")
    h = lax.axis_index("head")
    blocks = lax.axis_size("blk")
    x, z = h // 2, h % 2
    above = lax.rem(i + 1, blocks)
    below = lax.rem(i + blocks - 1, blocks)
    partners = [
        lax.rem(x + dx, 4) * 2 + lax.rem(z + dz, 2)
        for dx in (2, 1, 3, 0)
        for dz in (1, 0)
        if dx or dz
    ]

    barrier = pltpu.get_barrier_semaphore()
    for o in partners:
        pl.semaphore_signal(barrier, inc=1, device_id=(i, o), device_id_type=MESH)
    for b in (above, below):
        pl.semaphore_signal(barrier, inc=1, device_id=(b, h), device_id_type=MESH)

    loads = [
        pltpu.make_async_copy(o_hbm, o_rows, load_sem.at[0]),
        pltpu.make_async_copy(g_hbm, g_rows, load_sem.at[1]),
        pltpu.make_async_copy(seg_hbm, seg, load_sem.at[2]),
        pltpu.make_async_copy(order_hbm, order, load_sem.at[3]),
    ]
    for c in loads:
        c.start()

    def own_rows(o):
        return o // 4, pl.multiple_of(HALF + lax.rem(o, 4) * CHUNK, CHUNK)

    def cols(o, width):
        return pl.ds(pl.multiple_of(o * width, width), width)

    def piece(kind, target, source):
        s, row = own_rows(source)
        if kind == 0:
            return k_hbm.at[:, cols(target, HEAD)], k_all.at[s, pl.ds(row, CHUNK), :]
        if kind == 1:
            return v_hbm.at[:, cols(target, HEAD)], v_all.at[s, pl.ds(row, CHUNK), :]
        if kind == 2:
            return d_mine.at[target], d_all.at[source]
        if kind == 3:
            return q_hbm.at[:, cols(target, 2 * HEAD)], q_all.at[source]
        return g_hbm.at[:, cols(target, 2 * HEAD)], g_all.at[source]

    def send(kind, o):
        src, dst = piece(kind, o, h)
        return pltpu.make_async_remote_copy(
            src, dst, in_send.at[kind, o], in_recv.at[kind, h],
            device_id=(i, o), device_id_type=MESH,
        )

    def arrival(kind, o):
        src, dst = piece(kind, h, o)
        return pltpu.make_async_remote_copy(
            src, dst, in_send.at[kind, o], in_recv.at[kind, o],
            device_id=(i, o), device_id_type=MESH,
        )

    def own(kind):
        src, dst = piece(kind, h, h)
        return pltpu.make_async_copy(src, dst, own_sem.at[kind])

    for c in loads:
        c.wait()
    d_mine[...] = jnp.zeros_like(d_mine)
    for head in range(2 * GROUPS):
        at = slice(head * HEAD, (head + 1) * HEAD)
        product = o_rows[:, at].astype(F32) * g_rows[:, at].astype(F32)
        d_mine[head // 2, head % 2 : head % 2 + 1, :] = jnp.sum(
            product.T, axis=0, keepdims=True
        )

    mine = h // 4
    near = [mine * 4 + lax.rem(lax.rem(h, 4) + d, 4) for d in (1, 2, 3)]
    far = [(1 - mine) * 4 + lax.rem(lax.rem(h, 4) + d, 4) for d in (2, 3, 1, 0)]
    pl.semaphore_wait(barrier, GROUPS + 1)
    for kind in range(3):
        for o in partners:
            send(kind, o).start()
        own(kind).start()
    for group in (near, far):
        for kind in (3, 4):
            for o in group:
                send(kind, o).start()
            if group is near:
                own(kind).start()

    slot_half = [order[2 * i], order[2 * i + 1]]
    early = (slot_half[0] > slot_half[1]).astype(jnp.int32)
    is_early = [early == 0, early == 1]
    key_at = lax.broadcasted_iota(jnp.int32, (CHUNK, CHUNK), 0)
    row_at = lax.broadcasted_iota(jnp.int32, (CHUNK, CHUNK), 1)
    causal = key_at <= row_at
    for s in range(2):
        first = slot_half[s] * 4
        documents = []
        for c in range(8):
            line = seg[pl.ds(jnp.maximum(first - 4 + c, 0), 1), :].astype(F32)
            if c < 4:
                line = jnp.where(first == 0, -1.0, line)
            documents.append(line)
        for c in range(8):
            column = jnp.broadcast_to(documents[c], (CHUNK, CHUNK)).T
            for p in range(4):
                r = c - p
                if 0 <= r <= 4:
                    visible = column == documents[4 + p]
                    if r == 4:
                        visible = visible & causal
                    bias[s, p, r * CHUNK : (r + 1) * CHUNK, :] = jnp.where(
                        visible, 0.0, HIDDEN
                    )

    for kind in (0, 1):
        for o in partners:
            arrival(kind, o).wait_recv()
        own(kind).wait()
    late = 1 - early
    for n, slot in ((2, early), (3, late)):
        halo[n, 0] = k_all[slot, HALF:, :]
        halo[n, 1] = v_all[slot, HALF:, :]
    halo_up = pltpu.make_async_remote_copy(
        halo.at[2], halo.at[0], halo_send.at[0], halo_recv.at[0],
        device_id=(above, h), device_id_type=MESH,
    )
    halo_down = pltpu.make_async_remote_copy(
        halo.at[3], halo.at[1], halo_send.at[1], halo_recv.at[1],
        device_id=(below, h), device_id_type=MESH,
    )
    halo_up.start()
    halo_down.start()
    for s in range(2):
        kt_all[s, :, HALF:] = k_all[s, HALF:, :].T
    halo_up.wait_recv()
    halo_down.wait_recv()
    for s in range(2):
        at = jnp.where(is_early[s], 0, jnp.where(i == blocks - 1, 2, 1))
        before = halo[at, 0]
        k_all[s, :HALF, :] = before
        kt_all[s, :, :HALF] = before.T
        v_all[s, :HALF, :] = halo[at, 1]

    for o in partners:
        arrival(2, o).wait_recv()
    own(2).wait()

    def out_piece(kind, target, source):
        if kind == 0:
            return dq_stage.at[target], dq_out.at[:, cols(source, 2 * HEAD)]
        if kind == 1:
            return dk_stage.at[target], dk_out.at[:, cols(source, HEAD)]
        return dv_stage.at[target], dv_out.at[:, cols(source, HEAD)]

    def out_remote(kind, target, source, o):
        src, dst = out_piece(kind, target, source)
        return pltpu.make_async_remote_copy(
            src, dst, out_send.at[kind, target], out_recv.at[kind, source],
            device_id=(i, o), device_id_type=MESH,
        )

    def out_local(kind):
        src, dst = out_piece(kind, h, h)
        return pltpu.make_async_copy(src, dst, out_own.at[kind])

    def weigh(s, p):
        o = s * 4 + p
        window = slice(p * CHUNK, p * CHUNK + WINDOW)
        at = slice(p * 2 * CHUNK, (p + 1) * 2 * CHUNK)
        queries = jnp.concatenate([q_all[o, :, :HEAD], q_all[o, :, HEAD:]], axis=0)
        grads = jnp.concatenate([g_all[o, :, :HEAD], g_all[o, :, HEAD:]], axis=0)
        q_two[s, at, :] = queries
        g_two[s, at, :] = grads
        delta = jnp.concatenate([d_all[o, 0:1, :], d_all[o, 1:2, :]], axis=1)
        hide = bias[s, p]
        scores = lax.dot_general(k_all[s, window, :], queries, NT, preferred_element_type=F32)
        scores = scores * (SCALE * LOG2E) + jnp.concatenate([hide, hide], axis=1)
        top = jnp.max(scores, axis=0, keepdims=True)
        terms = jnp.exp2(scores - top)
        weights = terms * (1.0 / jnp.sum(terms, axis=0, keepdims=True))
        w_all[s, window, at] = weights.astype(BF16)
        pulls = lax.dot_general(v_all[s, window, :], grads, NT, preferred_element_type=F32)
        score_grads = (weights * (pulls - delta)).astype(BF16)
        s_all[s, window, at] = score_grads
        dq = jnp.dot(kt_all[s, :, window], score_grads, preferred_element_type=F32) * SCALE
        dq_stage[o, :, :HEAD] = dq[:, :HEAD].T.astype(BF16)
        dq_stage[o, :, HEAD:] = dq[:, HEAD:].T.astype(BF16)

    def key_terms(s, c):
        rows = slice(c * CHUNK, (c + 1) * CHUNK)
        at = slice(max(0, c - 4) * 2 * CHUNK, (min(3, c) + 1) * 2 * CHUNK)
        dv_sum[s, rows, :] = jnp.dot(
            w_all[s, rows, at], g_two[s, at, :], preferred_element_type=F32
        )
        dk_sum[s, rows, :] = jnp.dot(
            s_all[s, rows, at], q_two[s, at, :], preferred_element_type=F32
        )

    for kind in (3, 4):
        for o in near:
            arrival(kind, o).wait_recv()
        own(kind).wait()
    for p in range(4):
        weigh(mine, p)
    for o in near:
        out_remote(0, o, h, o).start()
    out_local(0).start()
    for c in range(8):
        key_terms(mine, c)

    for kind in (3, 4):
        for o in far:
            arrival(kind, o).wait_recv()
    for p in range(4):
        weigh(1 - mine, p)
        o = (1 - mine) * 4 + p
        out_remote(0, o, h, o).start()
    for c in range(8):
        key_terms(1 - mine, c)

    for n, slot in ((2, early), (3, late)):
        back[n, 0] = dk_sum[slot, :HALF, :].astype(BF16)
        back[n, 1] = dv_sum[slot, :HALF, :].astype(BF16)
    back_down = pltpu.make_async_remote_copy(
        back.at[2], back.at[1], back_send.at[0], back_recv.at[0],
        device_id=(below, h), device_id_type=MESH,
    )
    back_up = pltpu.make_async_remote_copy(
        back.at[3], back.at[0], back_send.at[1], back_recv.at[1],
        device_id=(above, h), device_id_type=MESH,
    )
    back_down.start()
    back_up.start()
    back_down.wait_recv()
    back_up.wait_recv()
    for s in range(2):
        at = jnp.where(is_early[s], jnp.where(i == blocks - 1, 3, 1), 0)
        nothing = jnp.logical_and(jnp.logical_not(is_early[s]), i == 0)
        for p in range(4):
            own_at = slice(HALF + p * CHUNK, HALF + (p + 1) * CHUNK)
            rows = slice(p * CHUNK, (p + 1) * CHUNK)
            dk_more = jnp.where(nothing, 0.0, back[at, 0, rows, :].astype(F32))
            dv_more = jnp.where(nothing, 0.0, back[at, 1, rows, :].astype(F32))
            dk_stage[s * 4 + p] = ((dk_sum[s, own_at, :] + dk_more) * SCALE).astype(BF16)
            dv_stage[s * 4 + p] = (dv_sum[s, own_at, :] + dv_more).astype(BF16)
    for kind in (1, 2):
        for o in partners:
            out_remote(kind, o, h, o).start()
        out_local(kind).start()

    halo_up.wait_send()
    halo_down.wait_send()
    back_down.wait_send()
    back_up.wait_send()
    for kind in range(KINDS):
        for o in partners:
            send(kind, o).wait_send()
    for kind in range(3):
        for o in partners:
            out_remote(kind, o, h, o).wait_send()
            out_remote(kind, h, o, o).wait_recv()
        out_local(kind).wait()


def local(queries, keys, values, outputs, out_grads, segment_ids, block_order):
    rows = queries.shape[0]
    hbm = pl.BlockSpec(memory_space=pltpu.HBM)
    dma = pltpu.SemaphoreType.DMA
    return pl.pallas_call(
        kernel,
        out_shape=[
            jax.ShapeDtypeStruct((rows, queries.shape[1]), BF16),
            jax.ShapeDtypeStruct((rows, keys.shape[1]), BF16),
            jax.ShapeDtypeStruct((rows, values.shape[1]), BF16),
        ],
        in_specs=[hbm] * 7,
        out_specs=[hbm] * 3,
        scratch_shapes=[
            pltpu.VMEM((segment_ids.shape[0] // CHUNK, CHUNK), jnp.int32),
            pltpu.SMEM(block_order.shape, jnp.int32),
            pltpu.VMEM((GROUPS, CHUNK, 2 * HEAD), BF16),
            pltpu.VMEM((GROUPS, CHUNK, 2 * HEAD), BF16),
            pltpu.VMEM((2, 2 * HALF, HEAD), BF16),
            pltpu.VMEM((2, 2 * HALF, HEAD), BF16),
            pltpu.VMEM((2, HEAD, 2 * HALF), BF16),
            pltpu.VMEM((GROUPS, 8, CHUNK), F32),
            pltpu.VMEM((GROUPS, 8, CHUNK), F32),
            pltpu.VMEM((CHUNK, 2 * GROUPS * HEAD), BF16),
            pltpu.VMEM((CHUNK, 2 * GROUPS * HEAD), BF16),
            pltpu.VMEM((2, 2 * HALF, HEAD), BF16),
            pltpu.VMEM((2, 2 * HALF, HEAD), BF16),
            pltpu.VMEM((2, 2 * HALF, 2 * HALF), BF16),
            pltpu.VMEM((2, 2 * HALF, 2 * HALF), BF16),
            pltpu.VMEM((4, 2, HALF, HEAD), BF16),
            pltpu.VMEM((4, 2, HALF, HEAD), BF16),
            pltpu.VMEM((2, 2 * HALF, HEAD), F32),
            pltpu.VMEM((2, 2 * HALF, HEAD), F32),
            pltpu.VMEM((GROUPS, CHUNK, 2 * HEAD), BF16),
            pltpu.VMEM((GROUPS, CHUNK, HEAD), BF16),
            pltpu.VMEM((GROUPS, CHUNK, HEAD), BF16),
            pltpu.VMEM((2, 4, WINDOW, CHUNK), F32),
            dma((4,)),
            dma((KINDS,)),
            dma((KINDS, GROUPS)),
            dma((KINDS, GROUPS)),
            dma((2,)),
            dma((2,)),
            dma((2,)),
            dma((2,)),
            dma((3, GROUPS)),
            dma((3, GROUPS)),
            dma((3,)),
        ],
        compiler_params=pltpu.CompilerParams(
            collective_id=0, has_side_effects=True, vmem_limit_bytes=60 * 1024 * 1024
        ),
        name="attention_backward",
    )(
        queries, keys, values, outputs, out_grads,
        segment_ids.reshape(-1, CHUNK), block_order,
    )


def solution(mesh):
    row = P(("blk", "head"), None)
    return jax.shard_map(
        local,
        mesh=mesh,
        in_specs=(row,) * 5 + (P(), P()),
        out_specs=(row,) * 3,
        check_vma=False,
    )
```

```python
import functools

import jax
import jax.numpy as jnp
from jax import lax
from jax.experimental import pallas as pl
from jax.experimental.pallas import tpu as pltpu
from jax.sharding import PartitionSpec as P

HEAD = 128
CHUNK = 128
HALF = 512
WINDOW = HALF + CHUNK
GROUPS = 8
SCALE = HEAD ** -0.5
LOG2E = 1.4426950408889634
HIDDEN = -1e30
MESH = pl.DeviceIdType.MESH
BF16 = jnp.bfloat16
F32 = jnp.float32
NT = (((1,), (1,)), ((), ()))
KINDS = 5


def kernel(
    q_hbm, k_hbm, v_hbm, o_hbm, g_hbm, seg_hbm, order_hbm,
    dq_out, dk_out, dv_out,
    seg, order, q_all, g_all, k_all, v_all, kt_all, d_all, d_mine, o_rows, g_rows,
    q_two, g_two, w_all, s_all,
    halo, back, dk_sum, dv_sum, dq_stage, dk_stage, dv_stage, bias,
    load_sem, own_sem, in_send, in_recv, halo_send, halo_recv, back_send, back_recv,
    out_send, out_recv, out_own,
):
    i = lax.axis_index("blk")
    h = lax.axis_index("head")
    blocks = lax.axis_size("blk")
    x, z = h // 2, h % 2
    has_above = i < blocks - 1
    has_below = i > 0
    above = jnp.minimum(i + 1, blocks - 1)
    below = jnp.maximum(i - 1, 0)
    partners = [
        lax.rem(x + dx, 4) * 2 + lax.rem(z + dz, 2)
        for dx in (2, 1, 3, 0)
        for dz in (1, 0)
        if dx or dz
    ]

    barrier = pltpu.get_barrier_semaphore()
    for o in partners:
        pl.semaphore_signal(barrier, inc=1, device_id=(i, o), device_id_type=MESH)
    for there, b in ((has_above, above), (has_below, below)):
        @pl.when(there)
        def _():
            pl.semaphore_signal(barrier, inc=1, device_id=(b, h), device_id_type=MESH)

    loads = [
        pltpu.make_async_copy(o_hbm, o_rows, load_sem.at[0]),
        pltpu.make_async_copy(g_hbm, g_rows, load_sem.at[1]),
        pltpu.make_async_copy(seg_hbm, seg, load_sem.at[2]),
        pltpu.make_async_copy(order_hbm, order, load_sem.at[3]),
    ]
    for c in loads:
        c.start()

    def own_rows(o):
        return o // 4, pl.multiple_of(HALF + lax.rem(o, 4) * CHUNK, CHUNK)

    def cols(o, width):
        return pl.ds(pl.multiple_of(o * width, width), width)

    def piece(kind, target, source):
        s, row = own_rows(source)
        if kind == 0:
            return k_hbm.at[:, cols(target, HEAD)], k_all.at[s, pl.ds(row, CHUNK), :]
        if kind == 1:
            return v_hbm.at[:, cols(target, HEAD)], v_all.at[s, pl.ds(row, CHUNK), :]
        if kind == 2:
            return d_mine.at[target], d_all.at[source]
        if kind == 3:
            return q_hbm.at[:, cols(target, 2 * HEAD)], q_all.at[source]
        return g_hbm.at[:, cols(target, 2 * HEAD)], g_all.at[source]

    def send(kind, o):
        src, dst = piece(kind, o, h)
        return pltpu.make_async_remote_copy(
            src, dst, in_send.at[kind, o], in_recv.at[kind, h],
            device_id=(i, o), device_id_type=MESH,
        )

    def arrival(kind, o):
        src, dst = piece(kind, h, o)
        return pltpu.make_async_remote_copy(
            src, dst, in_send.at[kind, o], in_recv.at[kind, o],
            device_id=(i, o), device_id_type=MESH,
        )

    def own(kind):
        src, dst = piece(kind, h, h)
        return pltpu.make_async_copy(src, dst, own_sem.at[kind])

    for c in loads:
        c.wait()
    d_mine[...] = jnp.zeros_like(d_mine)
    for head in range(2 * GROUPS):
        at = slice(head * HEAD, (head + 1) * HEAD)
        product = o_rows[:, at].astype(F32) * g_rows[:, at].astype(F32)
        d_mine[head // 2, head % 2 : head % 2 + 1, :] = jnp.sum(
            product.T, axis=0, keepdims=True
        )

    mine = h // 4
    near = [mine * 4 + lax.rem(lax.rem(h, 4) + d, 4) for d in (1, 2, 3)]
    far = [(1 - mine) * 4 + lax.rem(lax.rem(h, 4) + d, 4) for d in (2, 3, 1, 0)]
    pl.semaphore_wait(
        barrier, GROUPS - 1 + has_above.astype(jnp.int32) + has_below.astype(jnp.int32)
    )
    for kind in range(3):
        for o in partners:
            send(kind, o).start()
        own(kind).start()

    for group in (near, far):
        for kind in (3, 4):
            for o in group:
                send(kind, o).start()
            if group is near:
                own(kind).start()

    slot_half = [order[2 * i], order[2 * i + 1]]
    early = (slot_half[0] > slot_half[1]).astype(jnp.int32)
    is_early = [early == 0, early == 1]
    key_at = lax.broadcasted_iota(jnp.int32, (CHUNK, CHUNK), 0)
    row_at = lax.broadcasted_iota(jnp.int32, (CHUNK, CHUNK), 1)
    causal = key_at <= row_at
    for s in range(2):
        first = slot_half[s] * 4
        documents = []
        for c in range(8):
            line = seg[pl.ds(jnp.maximum(first - 4 + c, 0), 1), :].astype(F32)
            if c < 4:
                line = jnp.where(first == 0, -1.0, line)
            documents.append(line)
        for c in range(8):
            column = jnp.broadcast_to(documents[c], (CHUNK, CHUNK)).T
            for p in range(4):
                r = c - p
                if 0 <= r <= 4:
                    visible = column == documents[4 + p]
                    if r == 4:
                        visible = visible & causal
                    bias[s, p, r * CHUNK : (r + 1) * CHUNK, :] = jnp.where(
                        visible, 0.0, HIDDEN
                    )

    for kind in (0, 1):
        for o in partners:
            arrival(kind, o).wait_recv()
        own(kind).wait()
    late = 1 - early
    for n, slot in ((2, early), (3, late)):
        halo[n, 0] = k_all[slot, HALF:, :]
        halo[n, 1] = v_all[slot, HALF:, :]
    halo_up = pltpu.make_async_remote_copy(
        halo.at[2], halo.at[0], halo_send.at[0], halo_recv.at[0],
        device_id=(above, h), device_id_type=MESH,
    )
    halo_down = pltpu.make_async_remote_copy(
        halo.at[3], halo.at[1], halo_send.at[1], halo_recv.at[1],
        device_id=(below, h), device_id_type=MESH,
    )
    pl.when(has_above)(lambda: halo_up.start())
    pl.when(has_below)(lambda: halo_down.start())
    for s in range(2):
        kt_all[s, :, HALF:] = k_all[s, HALF:, :].T
    pl.when(has_below)(lambda: halo_up.wait_recv())
    pl.when(has_above)(lambda: halo_down.wait_recv())
    for s in range(2):
        at = jnp.where(is_early[s], jnp.where(has_below, 0, 2), jnp.where(has_above, 1, 2))
        before = halo[at, 0]
        k_all[s, :HALF, :] = before
        kt_all[s, :, :HALF] = before.T
        v_all[s, :HALF, :] = halo[at, 1]

    for o in partners:
        arrival(2, o).wait_recv()
    own(2).wait()

    def out_piece(kind, target, source):
        if kind == 0:
            return dq_stage.at[target], dq_out.at[:, cols(source, 2 * HEAD)]
        if kind == 1:
            return dk_stage.at[target], dk_out.at[:, cols(source, HEAD)]
        return dv_stage.at[target], dv_out.at[:, cols(source, HEAD)]

    def out_remote(kind, target, source, o):
        src, dst = out_piece(kind, target, source)
        return pltpu.make_async_remote_copy(
            src, dst, out_send.at[kind, target], out_recv.at[kind, source],
            device_id=(i, o), device_id_type=MESH,
        )

    def out_local(kind):
        src, dst = out_piece(kind, h, h)
        return pltpu.make_async_copy(src, dst, out_own.at[kind])

    def weigh(s, p):
        o = s * 4 + p
        window = slice(p * CHUNK, p * CHUNK + WINDOW)
        at = slice(p * 2 * CHUNK, (p + 1) * 2 * CHUNK)
        queries = jnp.concatenate([q_all[o, :, :HEAD], q_all[o, :, HEAD:]], axis=0)
        grads = jnp.concatenate([g_all[o, :, :HEAD], g_all[o, :, HEAD:]], axis=0)
        q_two[s, at, :] = queries
        g_two[s, at, :] = grads
        delta = jnp.concatenate([d_all[o, 0:1, :], d_all[o, 1:2, :]], axis=1)
        hide = bias[s, p]
        scores = lax.dot_general(k_all[s, window, :], queries, NT, preferred_element_type=F32)
        scores = scores * (SCALE * LOG2E) + jnp.concatenate([hide, hide], axis=1)
        top = jnp.max(scores, axis=0, keepdims=True)
        terms = jnp.exp2(scores - top)
        weights = terms * (1.0 / jnp.sum(terms, axis=0, keepdims=True))
        w_all[s, window, at] = weights.astype(BF16)
        pulls = lax.dot_general(v_all[s, window, :], grads, NT, preferred_element_type=F32)
        score_grads = (weights * (pulls - delta)).astype(BF16)
        s_all[s, window, at] = score_grads
        dq = jnp.dot(kt_all[s, :, window], score_grads, preferred_element_type=F32) * SCALE
        dq_stage[o, :, :HEAD] = dq[:, :HEAD].T.astype(BF16)
        dq_stage[o, :, HEAD:] = dq[:, HEAD:].T.astype(BF16)

    def key_terms(s, c):
        rows = slice(c * CHUNK, (c + 1) * CHUNK)
        at = slice(max(0, c - 4) * 2 * CHUNK, (min(3, c) + 1) * 2 * CHUNK)
        dv_sum[s, rows, :] = jnp.dot(
            w_all[s, rows, at], g_two[s, at, :], preferred_element_type=F32
        )
        dk_sum[s, rows, :] = jnp.dot(
            s_all[s, rows, at], q_two[s, at, :], preferred_element_type=F32
        )

    for kind in (3, 4):
        for o in near:
            arrival(kind, o).wait_recv()
        own(kind).wait()
    for p in range(4):
        weigh(mine, p)
    for o in near:
        out_remote(0, o, h, o).start()
    out_local(0).start()
    for c in range(8):
        key_terms(mine, c)

    for kind in (3, 4):
        for o in far:
            arrival(kind, o).wait_recv()
    for p in range(4):
        weigh(1 - mine, p)
    for c in range(4):
        key_terms(1 - mine, c)

    for n, slot in ((2, early), (3, late)):
        back[n, 0] = dk_sum[slot, :HALF, :].astype(BF16)
        back[n, 1] = dv_sum[slot, :HALF, :].astype(BF16)
    back_down = pltpu.make_async_remote_copy(
        back.at[2], back.at[1], back_send.at[0], back_recv.at[0],
        device_id=(below, h), device_id_type=MESH,
    )
    back_up = pltpu.make_async_remote_copy(
        back.at[3], back.at[0], back_send.at[1], back_recv.at[1],
        device_id=(above, h), device_id_type=MESH,
    )
    pl.when(has_below)(lambda: back_down.start())
    pl.when(has_above)(lambda: back_up.start())
    for o in far:
        out_remote(0, o, h, o).start()
    for c in range(4, 8):
        key_terms(1 - mine, c)
    pl.when(has_above)(lambda: back_down.wait_recv())
    pl.when(has_below)(lambda: back_up.wait_recv())
    for s in range(2):
        at = jnp.where(is_early[s], jnp.where(has_above, 1, 3), jnp.where(has_below, 0, 2))
        nothing = jnp.logical_not(jnp.logical_or(is_early[s], has_below))
        for p in range(4):
            own_at = slice(HALF + p * CHUNK, HALF + (p + 1) * CHUNK)
            rows = slice(p * CHUNK, (p + 1) * CHUNK)
            dk_more = jnp.where(nothing, 0.0, back[at, 0, rows, :].astype(F32))
            dv_more = jnp.where(nothing, 0.0, back[at, 1, rows, :].astype(F32))
            dk_stage[s * 4 + p] = ((dk_sum[s, own_at, :] + dk_more) * SCALE).astype(BF16)
            dv_stage[s * 4 + p] = (dv_sum[s, own_at, :] + dv_more).astype(BF16)
    for kind in (1, 2):
        for o in partners:
            out_remote(kind, o, h, o).start()
        out_local(kind).start()

    pl.when(has_above)(lambda: halo_up.wait_send())
    pl.when(has_below)(lambda: halo_down.wait_send())
    pl.when(has_below)(lambda: back_down.wait_send())
    pl.when(has_above)(lambda: back_up.wait_send())
    for kind in range(KINDS):
        for o in partners:
            send(kind, o).wait_send()
    for kind in range(3):
        for o in partners:
            out_remote(kind, o, h, o).wait_send()
            out_remote(kind, h, o, o).wait_recv()
        out_local(kind).wait()


def settle(dq_in, dk_in, dv_in, dq_out, dk_out, dv_out):
    dq_out[...] = dq_in[...]
    dk_out[...] = dk_in[...]
    dv_out[...] = dv_in[...]


def local(queries, keys, values, outputs, out_grads, segment_ids, block_order):
    hbm = pl.BlockSpec(memory_space=pltpu.HBM)
    dma = pltpu.SemaphoreType.DMA
    shapes = [jax.ShapeDtypeStruct(a.shape, BF16) for a in (queries, keys, values)]
    grads = pl.pallas_call(
        kernel,
        out_shape=shapes,
        in_specs=[hbm] * 7,
        out_specs=[hbm] * 3,
        scratch_shapes=[
            pltpu.VMEM((segment_ids.shape[0] // CHUNK, CHUNK), jnp.int32),
            pltpu.SMEM(block_order.shape, jnp.int32),
            pltpu.VMEM((GROUPS, CHUNK, 2 * HEAD), BF16),
            pltpu.VMEM((GROUPS, CHUNK, 2 * HEAD), BF16),
            pltpu.VMEM((2, 2 * HALF, HEAD), BF16),
            pltpu.VMEM((2, 2 * HALF, HEAD), BF16),
            pltpu.VMEM((2, HEAD, 2 * HALF), BF16),
            pltpu.VMEM((GROUPS, 8, CHUNK), F32),
            pltpu.VMEM((GROUPS, 8, CHUNK), F32),
            pltpu.VMEM((CHUNK, 2 * GROUPS * HEAD), BF16),
            pltpu.VMEM((CHUNK, 2 * GROUPS * HEAD), BF16),
            pltpu.VMEM((2, 2 * HALF, HEAD), BF16),
            pltpu.VMEM((2, 2 * HALF, HEAD), BF16),
            pltpu.VMEM((2, 2 * HALF, 2 * HALF), BF16),
            pltpu.VMEM((2, 2 * HALF, 2 * HALF), BF16),
            pltpu.VMEM((4, 2, HALF, HEAD), BF16),
            pltpu.VMEM((4, 2, HALF, HEAD), BF16),
            pltpu.VMEM((2, 2 * HALF, HEAD), F32),
            pltpu.VMEM((2, 2 * HALF, HEAD), F32),
            pltpu.VMEM((GROUPS, CHUNK, 2 * HEAD), BF16),
            pltpu.VMEM((GROUPS, CHUNK, HEAD), BF16),
            pltpu.VMEM((GROUPS, CHUNK, HEAD), BF16),
            pltpu.VMEM((2, 4, WINDOW, CHUNK), F32),
            dma((4,)),
            dma((KINDS,)),
            dma((KINDS, GROUPS)),
            dma((KINDS, GROUPS)),
            dma((2,)),
            dma((2,)),
            dma((2,)),
            dma((2,)),
            dma((3, GROUPS)),
            dma((3, GROUPS)),
            dma((3,)),
        ],
        compiler_params=pltpu.CompilerParams(
            collective_id=0, has_side_effects=True, vmem_limit_bytes=60 * 1024 * 1024
        ),
        name="attention_backward",
    )(
        queries, keys, values, outputs, out_grads,
        segment_ids.reshape(-1, CHUNK), block_order,
    )
    return pl.pallas_call(
        settle,
        out_shape=shapes,
        compiler_params=pltpu.CompilerParams(vmem_limit_bytes=60 * 1024 * 1024),
        name="settle",
    )(*grads)


def solution(mesh):
    row = P(("blk", "head"), None)
    return jax.shard_map(
        local,
        mesh=mesh,
        in_specs=(row,) * 5 + (P(), P()),
        out_specs=(row,) * 3,
        check_vma=False,
    )
```

```python
import functools

import jax
import jax.numpy as jnp
from jax import lax
from jax.experimental import pallas as pl
from jax.experimental.pallas import tpu as pltpu
from jax.sharding import PartitionSpec as P

HEAD = 128
CHUNK = 128
HALF = 512
WINDOW = HALF + CHUNK
GROUPS = 8
SCALE = HEAD ** -0.5
LOG2E = 1.4426950408889634
HIDDEN = -1e30
MESH = pl.DeviceIdType.MESH
BF16 = jnp.bfloat16
F32 = jnp.float32
NT = (((1,), (1,)), ((), ()))
KINDS = 5


def kernel(
    q_hbm, k_hbm, v_hbm, o_hbm, g_hbm, seg_hbm, order_hbm,
    dq_out, dk_out, dv_out,
    seg, order, q_all, g_all, k_all, v_all, kt_all, d_all, d_mine, o_rows, g_rows,
    q_two, g_two, w_all, s_all,
    halo, back_k, back_v, dk_sum, dv_sum, dq_stage, dk_stage, dv_stage, bias,
    load_sem, own_sem, in_send, in_recv, halo_send, halo_recv, back_send, back_recv,
    out_send, out_recv, out_own,
):
    i = lax.axis_index("blk")
    h = lax.axis_index("head")
    blocks = lax.axis_size("blk")
    x, z = h // 2, h % 2
    has_above = i < blocks - 1
    has_below = i > 0
    above = jnp.minimum(i + 1, blocks - 1)
    below = jnp.maximum(i - 1, 0)
    partners = [
        lax.rem(x + dx, 4) * 2 + lax.rem(z + dz, 2)
        for dx in (2, 1, 3, 0)
        for dz in (1, 0)
        if dx or dz
    ]

    barrier = pltpu.get_barrier_semaphore()
    for o in partners:
        pl.semaphore_signal(barrier, inc=1, device_id=(i, o), device_id_type=MESH)
    for there, b in ((has_above, above), (has_below, below)):
        @pl.when(there)
        def _():
            pl.semaphore_signal(barrier, inc=1, device_id=(b, h), device_id_type=MESH)

    loads = [
        pltpu.make_async_copy(o_hbm, o_rows, load_sem.at[0]),
        pltpu.make_async_copy(g_hbm, g_rows, load_sem.at[1]),
        pltpu.make_async_copy(seg_hbm, seg, load_sem.at[2]),
        pltpu.make_async_copy(order_hbm, order, load_sem.at[3]),
    ]
    for c in loads:
        c.start()

    def own_rows(o):
        return o // 4, pl.multiple_of(HALF + lax.rem(o, 4) * CHUNK, CHUNK)

    def cols(o, width):
        return pl.ds(pl.multiple_of(o * width, width), width)

    def piece(kind, target, source):
        s, row = own_rows(source)
        if kind == 0:
            return k_hbm.at[:, cols(target, HEAD)], k_all.at[s, pl.ds(row, CHUNK), :]
        if kind == 1:
            return v_hbm.at[:, cols(target, HEAD)], v_all.at[s, pl.ds(row, CHUNK), :]
        if kind == 2:
            return d_mine.at[target], d_all.at[source]
        if kind == 3:
            return q_hbm.at[:, cols(target, 2 * HEAD)], q_all.at[source]
        return g_hbm.at[:, cols(target, 2 * HEAD)], g_all.at[source]

    def send(kind, o):
        src, dst = piece(kind, o, h)
        return pltpu.make_async_remote_copy(
            src, dst, in_send.at[kind, o], in_recv.at[kind, h],
            device_id=(i, o), device_id_type=MESH,
        )

    def arrival(kind, o):
        src, dst = piece(kind, h, o)
        return pltpu.make_async_remote_copy(
            src, dst, in_send.at[kind, o], in_recv.at[kind, o],
            device_id=(i, o), device_id_type=MESH,
        )

    def own(kind):
        src, dst = piece(kind, h, h)
        return pltpu.make_async_copy(src, dst, own_sem.at[kind])

    for c in loads:
        c.wait()
    d_mine[...] = jnp.zeros_like(d_mine)
    for head in range(2 * GROUPS):
        at = slice(head * HEAD, (head + 1) * HEAD)
        product = o_rows[:, at].astype(F32) * g_rows[:, at].astype(F32)
        d_mine[head // 2, head % 2 : head % 2 + 1, :] = jnp.sum(
            product.T, axis=0, keepdims=True
        )

    mine = h // 4
    near = [mine * 4 + lax.rem(lax.rem(h, 4) + d, 4) for d in (1, 2, 3)]
    far = [(1 - mine) * 4 + lax.rem(lax.rem(h, 4) + d, 4) for d in (2, 3, 1, 0)]
    pl.semaphore_wait(
        barrier, GROUPS - 1 + has_above.astype(jnp.int32) + has_below.astype(jnp.int32)
    )
    for kind in range(3):
        for o in partners:
            send(kind, o).start()
        own(kind).start()

    for group in (near, far):
        for kind in (3, 4):
            for o in group:
                send(kind, o).start()
            if group is near:
                own(kind).start()

    slot_half = [order[2 * i], order[2 * i + 1]]
    early = (slot_half[0] > slot_half[1]).astype(jnp.int32)
    is_early = [early == 0, early == 1]
    key_at = lax.broadcasted_iota(jnp.int32, (CHUNK, CHUNK), 0)
    row_at = lax.broadcasted_iota(jnp.int32, (CHUNK, CHUNK), 1)
    causal = key_at <= row_at
    for s in range(2):
        first = slot_half[s] * 4
        documents = []
        for c in range(8):
            line = seg[pl.ds(jnp.maximum(first - 4 + c, 0), 1), :].astype(F32)
            if c < 4:
                line = jnp.where(first == 0, -1.0, line)
            documents.append(line)
        for c in range(8):
            column = jnp.broadcast_to(documents[c], (CHUNK, CHUNK)).T
            for p in range(4):
                r = c - p
                if 0 <= r <= 4:
                    visible = column == documents[4 + p]
                    if r == 4:
                        visible = visible & causal
                    bias[s, p, r * CHUNK : (r + 1) * CHUNK, :] = jnp.where(
                        visible, 0.0, HIDDEN
                    )

    for kind in (0, 1):
        for o in partners:
            arrival(kind, o).wait_recv()
        own(kind).wait()
    late = 1 - early
    for n, slot in ((2, early), (3, late)):
        halo[n, 0] = k_all[slot, HALF:, :]
        halo[n, 1] = v_all[slot, HALF:, :]
    halo_up = pltpu.make_async_remote_copy(
        halo.at[2], halo.at[0], halo_send.at[0], halo_recv.at[0],
        device_id=(above, h), device_id_type=MESH,
    )
    halo_down = pltpu.make_async_remote_copy(
        halo.at[3], halo.at[1], halo_send.at[1], halo_recv.at[1],
        device_id=(below, h), device_id_type=MESH,
    )
    pl.when(has_above)(lambda: halo_up.start())
    pl.when(has_below)(lambda: halo_down.start())
    for s in range(2):
        kt_all[s, :, HALF:] = k_all[s, HALF:, :].T
    pl.when(has_below)(lambda: halo_up.wait_recv())
    pl.when(has_above)(lambda: halo_down.wait_recv())
    for s in range(2):
        at = jnp.where(is_early[s], jnp.where(has_below, 0, 2), jnp.where(has_above, 1, 2))
        before = halo[at, 0]
        k_all[s, :HALF, :] = before
        kt_all[s, :, :HALF] = before.T
        v_all[s, :HALF, :] = halo[at, 1]

    for o in partners:
        arrival(2, o).wait_recv()
    own(2).wait()

    def out_piece(kind, target, source):
        if kind == 0:
            return dq_stage.at[target], dq_out.at[:, cols(source, 2 * HEAD)]
        if kind == 1:
            return dk_stage.at[target], dk_out.at[:, cols(source, HEAD)]
        return dv_stage.at[target], dv_out.at[:, cols(source, HEAD)]

    def out_remote(kind, target, source, o):
        src, dst = out_piece(kind, target, source)
        return pltpu.make_async_remote_copy(
            src, dst, out_send.at[kind, target], out_recv.at[kind, source],
            device_id=(i, o), device_id_type=MESH,
        )

    def out_local(kind):
        src, dst = out_piece(kind, h, h)
        return pltpu.make_async_copy(src, dst, out_own.at[kind])

    def weigh(s, p):
        o = s * 4 + p
        window = slice(p * CHUNK, p * CHUNK + WINDOW)
        at = slice(p * 2 * CHUNK, (p + 1) * 2 * CHUNK)
        queries = jnp.concatenate([q_all[o, :, :HEAD], q_all[o, :, HEAD:]], axis=0)
        grads = jnp.concatenate([g_all[o, :, :HEAD], g_all[o, :, HEAD:]], axis=0)
        q_two[s, at, :] = queries
        g_two[s, at, :] = grads
        delta = jnp.concatenate([d_all[o, 0:1, :], d_all[o, 1:2, :]], axis=1)
        hide = bias[s, p]
        scores = lax.dot_general(k_all[s, window, :], queries, NT, preferred_element_type=F32)
        scores = scores * (SCALE * LOG2E) + jnp.concatenate([hide, hide], axis=1)
        top = jnp.max(scores, axis=0, keepdims=True)
        terms = jnp.exp2(scores - top)
        weights = terms * (1.0 / jnp.sum(terms, axis=0, keepdims=True))
        w_all[s, window, at] = weights.astype(BF16)
        pulls = lax.dot_general(v_all[s, window, :], grads, NT, preferred_element_type=F32)
        score_grads = (weights * (pulls - delta)).astype(BF16)
        s_all[s, window, at] = score_grads
        dq = jnp.dot(kt_all[s, :, window], score_grads, preferred_element_type=F32) * SCALE
        dq_stage[o, :, :HEAD] = dq[:, :HEAD].T.astype(BF16)
        dq_stage[o, :, HEAD:] = dq[:, HEAD:].T.astype(BF16)

    def key_terms(s, c):
        rows = slice(c * CHUNK, (c + 1) * CHUNK)
        at = slice(max(0, c - 4) * 2 * CHUNK, (min(3, c) + 1) * 2 * CHUNK)
        dv_sum[s, rows, :] = jnp.dot(
            w_all[s, rows, at], g_two[s, at, :], preferred_element_type=F32
        )
        dk_sum[s, rows, :] = jnp.dot(
            s_all[s, rows, at], q_two[s, at, :], preferred_element_type=F32
        )

    for kind in (3, 4):
        for o in near:
            arrival(kind, o).wait_recv()
        own(kind).wait()
    for p in range(4):
        weigh(mine, p)
    for o in near:
        out_remote(0, o, h, o).start()
    out_local(0).start()
    for c in range(8):
        key_terms(mine, c)

    for kind in (3, 4):
        for o in far:
            arrival(kind, o).wait_recv()
    for p in range(4):
        weigh(1 - mine, p)
    for c in range(4):
        key_terms(1 - mine, c)

    for n, slot in ((2, early), (3, late)):
        back_k[n] = dk_sum[slot, :HALF, :].astype(BF16)
        back_v[n] = dv_sum[slot, :HALF, :].astype(BF16)
    back_down, back_up = {}, {}
    for n, back in ((1, back_v), (0, back_k)):
        back_down[n] = pltpu.make_async_remote_copy(
            back.at[2], back.at[1], back_send.at[0, n], back_recv.at[0, n],
            device_id=(below, h), device_id_type=MESH,
        )
        back_up[n] = pltpu.make_async_remote_copy(
            back.at[3], back.at[0], back_send.at[1, n], back_recv.at[1, n],
            device_id=(above, h), device_id_type=MESH,
        )
        pl.when(has_below)(lambda: back_down[n].start())
        pl.when(has_above)(lambda: back_up[n].start())
    for o in far:
        out_remote(0, o, h, o).start()
    for c in range(4, 8):
        key_terms(1 - mine, c)
    for n, back, total, stage, scale in (
        (1, back_v, dv_sum, dv_stage, 1.0),
        (0, back_k, dk_sum, dk_stage, SCALE),
    ):
        pl.when(has_above)(lambda: back_down[n].wait_recv())
        pl.when(has_below)(lambda: back_up[n].wait_recv())
        for s in range(2):
            at = jnp.where(is_early[s], jnp.where(has_above, 1, 3), jnp.where(has_below, 0, 2))
            nothing = jnp.logical_not(jnp.logical_or(is_early[s], has_below))
            for p in range(4):
                own_at = slice(HALF + p * CHUNK, HALF + (p + 1) * CHUNK)
                rows = slice(p * CHUNK, (p + 1) * CHUNK)
                more = jnp.where(nothing, 0.0, back[at, rows, :].astype(F32))
                stage[s * 4 + p] = ((total[s, own_at, :] + more) * scale).astype(BF16)
        for o in partners:
            out_remote(2 if n else 1, o, h, o).start()
        out_local(2 if n else 1).start()

    pl.when(has_above)(lambda: halo_up.wait_send())
    pl.when(has_below)(lambda: halo_down.wait_send())
    for n in (0, 1):
        pl.when(has_below)(lambda: back_down[n].wait_send())
        pl.when(has_above)(lambda: back_up[n].wait_send())
    for kind in range(KINDS):
        for o in partners:
            send(kind, o).wait_send()
    for kind in range(3):
        for o in partners:
            out_remote(kind, o, h, o).wait_send()
            out_remote(kind, h, o, o).wait_recv()
        out_local(kind).wait()


def settle(dq_in, dk_in, dv_in, dq_out, dk_out, dv_out, dq_mid, dk_mid, dv_mid, sem):
    trios = []
    for a, m, b in ((dq_in, dq_mid, dq_out), (dk_in, dk_mid, dk_out), (dv_in, dv_mid, dv_out)):
        for part in range(2):
            rows = pl.ds(part * 64, 64)
            trios.append((a.at[rows, :], m.at[rows, :], b.at[rows, :]))
    ins = [pltpu.make_async_copy(a, m, sem.at[0, n]) for n, (a, m, _) in enumerate(trios)]
    outs = [pltpu.make_async_copy(m, b, sem.at[1, n]) for n, (_, m, b) in enumerate(trios)]
    for c in ins:
        c.start()
    for c, d in zip(ins, outs):
        c.wait()
        d.start()
    for d in outs:
        d.wait()


def local(queries, keys, values, outputs, out_grads, segment_ids, block_order):
    hbm = pl.BlockSpec(memory_space=pltpu.HBM)
    dma = pltpu.SemaphoreType.DMA
    shapes = [jax.ShapeDtypeStruct(a.shape, BF16) for a in (queries, keys, values)]
    grads = pl.pallas_call(
        kernel,
        out_shape=shapes,
        in_specs=[hbm] * 7,
        out_specs=[hbm] * 3,
        scratch_shapes=[
            pltpu.VMEM((segment_ids.shape[0] // CHUNK, CHUNK), jnp.int32),
            pltpu.SMEM(block_order.shape, jnp.int32),
            pltpu.VMEM((GROUPS, CHUNK, 2 * HEAD), BF16),
            pltpu.VMEM((GROUPS, CHUNK, 2 * HEAD), BF16),
            pltpu.VMEM((2, 2 * HALF, HEAD), BF16),
            pltpu.VMEM((2, 2 * HALF, HEAD), BF16),
            pltpu.VMEM((2, HEAD, 2 * HALF), BF16),
            pltpu.VMEM((GROUPS, 8, CHUNK), F32),
            pltpu.VMEM((GROUPS, 8, CHUNK), F32),
            pltpu.VMEM((CHUNK, 2 * GROUPS * HEAD), BF16),
            pltpu.VMEM((CHUNK, 2 * GROUPS * HEAD), BF16),
            pltpu.VMEM((2, 2 * HALF, HEAD), BF16),
            pltpu.VMEM((2, 2 * HALF, HEAD), BF16),
            pltpu.VMEM((2, 2 * HALF, 2 * HALF), BF16),
            pltpu.VMEM((2, 2 * HALF, 2 * HALF), BF16),
            pltpu.VMEM((4, 2, HALF, HEAD), BF16),
            pltpu.VMEM((4, HALF, HEAD), BF16),
            pltpu.VMEM((4, HALF, HEAD), BF16),
            pltpu.VMEM((2, 2 * HALF, HEAD), F32),
            pltpu.VMEM((2, 2 * HALF, HEAD), F32),
            pltpu.VMEM((GROUPS, CHUNK, 2 * HEAD), BF16),
            pltpu.VMEM((GROUPS, CHUNK, HEAD), BF16),
            pltpu.VMEM((GROUPS, CHUNK, HEAD), BF16),
            pltpu.VMEM((2, 4, WINDOW, CHUNK), F32),
            dma((4,)),
            dma((KINDS,)),
            dma((KINDS, GROUPS)),
            dma((KINDS, GROUPS)),
            dma((2,)),
            dma((2,)),
            dma((2, 2)),
            dma((2, 2)),
            dma((3, GROUPS)),
            dma((3, GROUPS)),
            dma((3,)),
        ],
        compiler_params=pltpu.CompilerParams(
            collective_id=0, has_side_effects=True, vmem_limit_bytes=60 * 1024 * 1024
        ),
        name="attention_backward",
    )(
        queries, keys, values, outputs, out_grads,
        segment_ids.reshape(-1, CHUNK), block_order,
    )
    return pl.pallas_call(
        settle,
        out_shape=shapes,
        in_specs=[hbm] * 3,
        out_specs=[hbm] * 3,
        scratch_shapes=[pltpu.VMEM(a.shape, BF16) for a in shapes] + [dma((2, 6))],
        compiler_params=pltpu.CompilerParams(vmem_limit_bytes=60 * 1024 * 1024),
        name="settle",
    )(*grads)


def solution(mesh):
    row = P(("blk", "head"), None)
    return jax.shard_map(
        local,
        mesh=mesh,
        in_specs=(row,) * 5 + (P(), P()),
        out_specs=(row,) * 3,
        check_vma=False,
    )
```

```python
import functools

import jax
import jax.numpy as jnp
from jax import lax
from jax.experimental import pallas as pl
from jax.experimental.pallas import tpu as pltpu
from jax.sharding import PartitionSpec as P

HEAD = 128
CHUNK = 128
HALF = 512
WINDOW = HALF + CHUNK
GROUPS = 8
SCALE = HEAD ** -0.5
LOG2E = 1.4426950408889634
HIDDEN = -1e30
MESH = pl.DeviceIdType.MESH
BF16 = jnp.bfloat16
F32 = jnp.float32
NT = (((1,), (1,)), ((), ()))
KINDS = 5


def kernel(
    q_hbm, k_hbm, v_hbm, o_hbm, g_hbm, seg_hbm, order_hbm,
    dq_out, dk_out, dv_out,
    seg, order, q_all, g_all, k_all, v_all, kt_all, d_all, d_mine, o_rows, g_rows,
    q_two, g_two, w_all, s_all,
    halo_k, halo_v, back_k, back_v, dk_sum, dv_sum, dq_stage, dk_stage, dv_stage, bias,
    load_sem, own_sem, in_send, in_recv, halo_send, halo_recv, back_send, back_recv,
    out_send, out_recv, out_own,
):
    i = lax.axis_index("blk")
    h = lax.axis_index("head")
    blocks = lax.axis_size("blk")
    x, z = h // 2, h % 2
    has_above = i < blocks - 1
    has_below = i > 0
    above = jnp.minimum(i + 1, blocks - 1)
    below = jnp.maximum(i - 1, 0)
    partners = [
        lax.rem(x + dx, 4) * 2 + lax.rem(z + dz, 2)
        for dx in (2, 1, 3, 0)
        for dz in (1, 0)
        if dx or dz
    ]

    barrier = pltpu.get_barrier_semaphore()
    for o in partners:
        pl.semaphore_signal(barrier, inc=1, device_id=(i, o), device_id_type=MESH)
    for there, b in ((has_above, above), (has_below, below)):
        @pl.when(there)
        def _():
            pl.semaphore_signal(barrier, inc=1, device_id=(b, h), device_id_type=MESH)

    loads = [
        pltpu.make_async_copy(o_hbm, o_rows, load_sem.at[0]),
        pltpu.make_async_copy(g_hbm, g_rows, load_sem.at[1]),
        pltpu.make_async_copy(seg_hbm, seg, load_sem.at[2]),
        pltpu.make_async_copy(order_hbm, order, load_sem.at[3]),
    ]
    for c in loads:
        c.start()

    def own_rows(o):
        return o // 4, pl.multiple_of(HALF + lax.rem(o, 4) * CHUNK, CHUNK)

    def cols(o, width):
        return pl.ds(pl.multiple_of(o * width, width), width)

    def piece(kind, target, source):
        s, row = own_rows(source)
        if kind == 0:
            return k_hbm.at[:, cols(target, HEAD)], k_all.at[s, pl.ds(row, CHUNK), :]
        if kind == 1:
            return v_hbm.at[:, cols(target, HEAD)], v_all.at[s, pl.ds(row, CHUNK), :]
        if kind == 2:
            return d_mine.at[target], d_all.at[source]
        if kind == 3:
            return q_hbm.at[:, cols(target, 2 * HEAD)], q_all.at[source]
        return g_hbm.at[:, cols(target, 2 * HEAD)], g_all.at[source]

    def send(kind, o):
        src, dst = piece(kind, o, h)
        return pltpu.make_async_remote_copy(
            src, dst, in_send.at[kind, o], in_recv.at[kind, h],
            device_id=(i, o), device_id_type=MESH,
        )

    def arrival(kind, o):
        src, dst = piece(kind, h, o)
        return pltpu.make_async_remote_copy(
            src, dst, in_send.at[kind, o], in_recv.at[kind, o],
            device_id=(i, o), device_id_type=MESH,
        )

    def own(kind):
        src, dst = piece(kind, h, h)
        return pltpu.make_async_copy(src, dst, own_sem.at[kind])

    for c in loads:
        c.wait()
    d_mine[...] = jnp.zeros_like(d_mine)
    for head in range(2 * GROUPS):
        at = slice(head * HEAD, (head + 1) * HEAD)
        product = o_rows[:, at].astype(F32) * g_rows[:, at].astype(F32)
        d_mine[head // 2, head % 2 : head % 2 + 1, :] = jnp.sum(
            product.T, axis=0, keepdims=True
        )

    mine = h // 4
    near = [mine * 4 + lax.rem(lax.rem(h, 4) + d, 4) for d in (1, 2, 3)]
    far = [(1 - mine) * 4 + lax.rem(lax.rem(h, 4) + d, 4) for d in (2, 3, 1, 0)]
    pl.semaphore_wait(
        barrier, GROUPS - 1 + has_above.astype(jnp.int32) + has_below.astype(jnp.int32)
    )
    for kind in range(3):
        for o in partners:
            send(kind, o).start()
        own(kind).start()

    for group in (near, far):
        for kind in (3, 4):
            for o in group:
                send(kind, o).start()
            if group is near:
                own(kind).start()

    slot_half = [order[2 * i], order[2 * i + 1]]
    early = (slot_half[0] > slot_half[1]).astype(jnp.int32)
    is_early = [early == 0, early == 1]
    key_at = lax.broadcasted_iota(jnp.int32, (CHUNK, CHUNK), 0)
    row_at = lax.broadcasted_iota(jnp.int32, (CHUNK, CHUNK), 1)
    causal = key_at <= row_at
    for s in range(2):
        first = slot_half[s] * 4
        documents = []
        for c in range(8):
            line = seg[pl.ds(jnp.maximum(first - 4 + c, 0), 1), :].astype(F32)
            if c < 4:
                line = jnp.where(first == 0, -1.0, line)
            documents.append(line)
        for c in range(8):
            column = jnp.broadcast_to(documents[c], (CHUNK, CHUNK)).T
            for p in range(4):
                r = c - p
                if 0 <= r <= 4:
                    visible = column == documents[4 + p]
                    if r == 4:
                        visible = visible & causal
                    bias[s, p, r * CHUNK : (r + 1) * CHUNK, :] = jnp.where(
                        visible, 0.0, HIDDEN
                    )

    late = 1 - early
    halo_up, halo_down = {}, {}
    for n, halo, rows in ((0, halo_k, k_all), (1, halo_v, v_all)):
        for o in partners:
            arrival(n, o).wait_recv()
        own(n).wait()
        for m, slot in ((2, early), (3, late)):
            halo[m] = rows[slot, HALF:, :]
        halo_up[n] = pltpu.make_async_remote_copy(
            halo.at[2], halo.at[0], halo_send.at[0, n], halo_recv.at[0, n],
            device_id=(above, h), device_id_type=MESH,
        )
        halo_down[n] = pltpu.make_async_remote_copy(
            halo.at[3], halo.at[1], halo_send.at[1, n], halo_recv.at[1, n],
            device_id=(below, h), device_id_type=MESH,
        )
        pl.when(has_above)(lambda: halo_up[n].start())
        pl.when(has_below)(lambda: halo_down[n].start())
    for s in range(2):
        kt_all[s, :, HALF:] = k_all[s, HALF:, :].T
    for n, halo, rows in ((0, halo_k, k_all), (1, halo_v, v_all)):
        pl.when(has_below)(lambda: halo_up[n].wait_recv())
        pl.when(has_above)(lambda: halo_down[n].wait_recv())
        for s in range(2):
            at = jnp.where(is_early[s], jnp.where(has_below, 0, 2), jnp.where(has_above, 1, 2))
            before = halo[at]
            rows[s, :HALF, :] = before
            if n == 0:
                kt_all[s, :, :HALF] = before.T

    for o in partners:
        arrival(2, o).wait_recv()
    own(2).wait()

    def out_piece(kind, target, source):
        if kind == 0:
            return dq_stage.at[target], dq_out.at[:, cols(source, 2 * HEAD)]
        if kind == 1:
            return dk_stage.at[target], dk_out.at[:, cols(source, HEAD)]
        return dv_stage.at[target], dv_out.at[:, cols(source, HEAD)]

    def out_remote(kind, target, source, o):
        src, dst = out_piece(kind, target, source)
        return pltpu.make_async_remote_copy(
            src, dst, out_send.at[kind, target], out_recv.at[kind, source],
            device_id=(i, o), device_id_type=MESH,
        )

    def out_local(kind):
        src, dst = out_piece(kind, h, h)
        return pltpu.make_async_copy(src, dst, out_own.at[kind])

    def weigh(s, p):
        o = s * 4 + p
        window = slice(p * CHUNK, p * CHUNK + WINDOW)
        at = slice(p * 2 * CHUNK, (p + 1) * 2 * CHUNK)
        queries = jnp.concatenate([q_all[o, :, :HEAD], q_all[o, :, HEAD:]], axis=0)
        grads = jnp.concatenate([g_all[o, :, :HEAD], g_all[o, :, HEAD:]], axis=0)
        q_two[s, at, :] = queries
        g_two[s, at, :] = grads
        delta = jnp.concatenate([d_all[o, 0:1, :], d_all[o, 1:2, :]], axis=1)
        hide = bias[s, p]
        scores = lax.dot_general(k_all[s, window, :], queries, NT, preferred_element_type=F32)
        scores = scores * (SCALE * LOG2E) + jnp.concatenate([hide, hide], axis=1)
        top = jnp.max(scores, axis=0, keepdims=True)
        terms = jnp.exp2(scores - top)
        weights = terms * (1.0 / jnp.sum(terms, axis=0, keepdims=True))
        w_all[s, window, at] = weights.astype(BF16)
        pulls = lax.dot_general(v_all[s, window, :], grads, NT, preferred_element_type=F32)
        score_grads = (weights * (pulls - delta)).astype(BF16)
        s_all[s, window, at] = score_grads
        dq = jnp.dot(kt_all[s, :, window], score_grads, preferred_element_type=F32) * SCALE
        dq_stage[o, :, :HEAD] = dq[:, :HEAD].T.astype(BF16)
        dq_stage[o, :, HEAD:] = dq[:, HEAD:].T.astype(BF16)

    def key_terms(n, s, c):
        total, parts, rows_two = ((dk_sum, s_all, q_two), (dv_sum, w_all, g_two))[n]
        rows = slice(c * CHUNK, (c + 1) * CHUNK)
        at = slice(max(0, c - 4) * 2 * CHUNK, (min(3, c) + 1) * 2 * CHUNK)
        total[s, rows, :] = jnp.dot(
            parts[s, rows, at], rows_two[s, at, :], preferred_element_type=F32
        )

    for kind in (3, 4):
        for o in near:
            arrival(kind, o).wait_recv()
        own(kind).wait()
    for p in range(4):
        weigh(mine, p)
    for o in near:
        out_remote(0, o, h, o).start()
    out_local(0).start()
    for n in (1, 0):
        for c in range(8):
            key_terms(n, mine, c)

    for kind in (3, 4):
        for o in far:
            arrival(kind, o).wait_recv()
    for p in range(4):
        weigh(1 - mine, p)
    back_down, back_up = {}, {}
    for n, back, total in ((1, back_v, dv_sum), (0, back_k, dk_sum)):
        for c in range(4):
            key_terms(n, 1 - mine, c)
        for m, slot in ((2, early), (3, late)):
            back[m] = total[slot, :HALF, :].astype(BF16)
        back_down[n] = pltpu.make_async_remote_copy(
            back.at[2], back.at[1], back_send.at[0, n], back_recv.at[0, n],
            device_id=(below, h), device_id_type=MESH,
        )
        back_up[n] = pltpu.make_async_remote_copy(
            back.at[3], back.at[0], back_send.at[1, n], back_recv.at[1, n],
            device_id=(above, h), device_id_type=MESH,
        )
        pl.when(has_below)(lambda: back_down[n].start())
        pl.when(has_above)(lambda: back_up[n].start())
    for o in far:
        out_remote(0, o, h, o).start()
    for n in (1, 0):
        for c in range(4, 8):
            key_terms(n, 1 - mine, c)
    for n, back, total, stage, scale in (
        (1, back_v, dv_sum, dv_stage, 1.0),
        (0, back_k, dk_sum, dk_stage, SCALE),
    ):
        pl.when(has_above)(lambda: back_down[n].wait_recv())
        pl.when(has_below)(lambda: back_up[n].wait_recv())
        for s in range(2):
            at = jnp.where(is_early[s], jnp.where(has_above, 1, 3), jnp.where(has_below, 0, 2))
            nothing = jnp.logical_not(jnp.logical_or(is_early[s], has_below))
            for p in range(4):
                own_at = slice(HALF + p * CHUNK, HALF + (p + 1) * CHUNK)
                rows = slice(p * CHUNK, (p + 1) * CHUNK)
                more = jnp.where(nothing, 0.0, back[at, rows, :].astype(F32))
                stage[s * 4 + p] = ((total[s, own_at, :] + more) * scale).astype(BF16)
        for o in partners:
            out_remote(2 if n else 1, o, h, o).start()
        out_local(2 if n else 1).start()

    for n in (0, 1):
        pl.when(has_above)(lambda: halo_up[n].wait_send())
        pl.when(has_below)(lambda: halo_down[n].wait_send())
        pl.when(has_below)(lambda: back_down[n].wait_send())
        pl.when(has_above)(lambda: back_up[n].wait_send())
    for kind in range(KINDS):
        for o in partners:
            send(kind, o).wait_send()
    for kind in range(3):
        for o in partners:
            out_remote(kind, o, h, o).wait_send()
            out_remote(kind, h, o, o).wait_recv()
        out_local(kind).wait()


def settle(dq_in, dk_in, dv_in, dq_out, dk_out, dv_out, dq_mid, dk_mid, dv_mid, sem):
    trios = []
    for a, m, b in ((dq_in, dq_mid, dq_out), (dk_in, dk_mid, dk_out), (dv_in, dv_mid, dv_out)):
        for part in range(2):
            rows = pl.ds(part * 64, 64)
            trios.append((a.at[rows, :], m.at[rows, :], b.at[rows, :]))
    ins = [pltpu.make_async_copy(a, m, sem.at[0, n]) for n, (a, m, _) in enumerate(trios)]
    outs = [pltpu.make_async_copy(m, b, sem.at[1, n]) for n, (_, m, b) in enumerate(trios)]
    for c in ins:
        c.start()
    for c, d in zip(ins, outs):
        c.wait()
        d.start()
    for d in outs:
        d.wait()


def local(queries, keys, values, outputs, out_grads, segment_ids, block_order):
    hbm = pl.BlockSpec(memory_space=pltpu.HBM)
    dma = pltpu.SemaphoreType.DMA
    shapes = [jax.ShapeDtypeStruct(a.shape, BF16) for a in (queries, keys, values)]
    grads = pl.pallas_call(
        kernel,
        out_shape=shapes,
        in_specs=[hbm] * 7,
        out_specs=[hbm] * 3,
        scratch_shapes=[
            pltpu.VMEM((segment_ids.shape[0] // CHUNK, CHUNK), jnp.int32),
            pltpu.SMEM(block_order.shape, jnp.int32),
            pltpu.VMEM((GROUPS, CHUNK, 2 * HEAD), BF16),
            pltpu.VMEM((GROUPS, CHUNK, 2 * HEAD), BF16),
            pltpu.VMEM((2, 2 * HALF, HEAD), BF16),
            pltpu.VMEM((2, 2 * HALF, HEAD), BF16),
            pltpu.VMEM((2, HEAD, 2 * HALF), BF16),
            pltpu.VMEM((GROUPS, 8, CHUNK), F32),
            pltpu.VMEM((GROUPS, 8, CHUNK), F32),
            pltpu.VMEM((CHUNK, 2 * GROUPS * HEAD), BF16),
            pltpu.VMEM((CHUNK, 2 * GROUPS * HEAD), BF16),
            pltpu.VMEM((2, 2 * HALF, HEAD), BF16),
            pltpu.VMEM((2, 2 * HALF, HEAD), BF16),
            pltpu.VMEM((2, 2 * HALF, 2 * HALF), BF16),
            pltpu.VMEM((2, 2 * HALF, 2 * HALF), BF16),
            pltpu.VMEM((4, HALF, HEAD), BF16),
            pltpu.VMEM((4, HALF, HEAD), BF16),
            pltpu.VMEM((4, HALF, HEAD), BF16),
            pltpu.VMEM((4, HALF, HEAD), BF16),
            pltpu.VMEM((2, 2 * HALF, HEAD), F32),
            pltpu.VMEM((2, 2 * HALF, HEAD), F32),
            pltpu.VMEM((GROUPS, CHUNK, 2 * HEAD), BF16),
            pltpu.VMEM((GROUPS, CHUNK, HEAD), BF16),
            pltpu.VMEM((GROUPS, CHUNK, HEAD), BF16),
            pltpu.VMEM((2, 4, WINDOW, CHUNK), F32),
            dma((4,)),
            dma((KINDS,)),
            dma((KINDS, GROUPS)),
            dma((KINDS, GROUPS)),
            dma((2, 2)),
            dma((2, 2)),
            dma((2, 2)),
            dma((2, 2)),
            dma((3, GROUPS)),
            dma((3, GROUPS)),
            dma((3,)),
        ],
        compiler_params=pltpu.CompilerParams(
            collective_id=0, has_side_effects=True, vmem_limit_bytes=60 * 1024 * 1024
        ),
        name="attention_backward",
    )(
        queries, keys, values, outputs, out_grads,
        segment_ids.reshape(-1, CHUNK), block_order,
    )
    return pl.pallas_call(
        settle,
        out_shape=shapes,
        in_specs=[hbm] * 3,
        out_specs=[hbm] * 3,
        scratch_shapes=[pltpu.VMEM(a.shape, BF16) for a in shapes] + [dma((2, 6))],
        compiler_params=pltpu.CompilerParams(vmem_limit_bytes=60 * 1024 * 1024),
        name="settle",
    )(*grads)


def solution(mesh):
    row = P(("blk", "head"), None)
    return jax.shard_map(
        local,
        mesh=mesh,
        in_specs=(row,) * 5 + (P(), P()),
        out_specs=(row,) * 3,
        check_vma=False,
    )
```
